512 devices in a mesh: seq: 128 (over z, y, core), ch: 4 (over x).
Axes of the slice: x: 4, y: 4, z: 16, core: 2. Of those that a mesh axis runs over, the one named last changes fastest.
Arguments:
- ingest: bfloat16 [131072, 4096], P('seq', 'ch'), may hold values from -6 to 6
- ingest_count: int32 [128], P('seq'), may hold values from 0 to 1024, as said below
- doc_lengths: int32 [128], replicated, may hold values from 1 to 2048, as said below
- in_weight: bfloat16 [4096, 5120], P('seq', 'ch'), may hold values from -0.09375 to 0.09375
- conv_weight: float32 [4, 5120], P(None, 'ch'), may hold values from -3 to 3
- conv_bias: float32 [5120], P('ch'), may hold values from -3 to 3
Outputs:
- conv_out: bfloat16 [65536, 5120], P('seq', 'ch')
The draws below stay inside these ranges and needn't reach their ends.
Inputs may be any that keep to these rules, and one draw needn't show every extreme that they name: Device i keeps its valid rows in its first ingest_count[i] slots; the devices before i together hold between i * 512 - 256 and i * 512 + 256 rows, both ends reached in every draw; the first device holds 511 rows, and all devices together hold 65536 rows. `doc_lengths`: the lengths sum to 65536; the first document has exactly 2048 tokens.
All inputs are finite; a program needn't handle non-finite values.
Results may differ from the reference program's by a relative error of at most 0.012.
Values may be sent and summed in bfloat16 or wider, within the bound.
A program may use at most 128 MiB of HBM per device.

```python
import jax
import jax.numpy as jnp
from jax import lax

D = 4096
CH = 5120
TAPS = 4
TOK_DEV = 512
CAP = 1024
TOKENS = 65536
LONGEST = 2048
N_SEQ = 128


def draw_ingest_count(key, part):
    key = jax.random.fold_in(key, 11)
    first_key, second_key = jax.random.split(key)
    half = TOK_DEV // 2
    inner = jax.random.randint(first_key, (N_SEQ - 1,), -half, half + 1)
    chosen = jax.random.randint(second_key, (), 2, N_SEQ - 1)
    places = jnp.arange(N_SEQ - 1)
    inner = jnp.where(places == chosen, half, jnp.where(places == chosen - 1, -half, inner))
    inner = jnp.where(places == 0, -1, inner)
    edges = jnp.concatenate([jnp.zeros((1,), jnp.int32), inner.astype(jnp.int32), jnp.zeros((1,), jnp.int32)])
    return (TOK_DEV + edges[1:] - edges[:-1]).astype(jnp.int32)


def draw_doc_lengths(key, part):
    key = jax.random.fold_in(key, 13)
    others = N_SEQ - 1
    remaining = (N_SEQ - 4) * TOK_DEV
    share = remaining // others
    extra_ones = remaining - share * others
    places = jnp.arange(others, dtype=jnp.int32)
    base = share + (places < extra_ones).astype(jnp.int32)
    pairs = others // 2
    moves = jax.random.randint(key, (pairs,), -(share - 1), share)
    delta = jnp.zeros((others,), jnp.int32)
    delta = delta.at[0:2 * pairs:2].add(moves.astype(jnp.int32))
    delta = delta.at[1:2 * pairs:2].add(-moves.astype(jnp.int32))
    rest = base + delta
    first = jnp.full((1,), LONGEST, jnp.int32)
    return jnp.concatenate([first, rest]).astype(jnp.int32)


def levels(own_key, dims, pieces, low, high):
    factor_of, own = 1.0, jax.random.fold_in(own_key, 6)
    for axis_at, shards_of in pieces:
        draws = jnp.exp(jax.random.uniform(jax.random.fold_in(own, axis_at), (shards_of,), jnp.float32, low / len(pieces), high / len(pieces)))
        factor_of = factor_of * jnp.repeat(draws, dims[axis_at] // shards_of).reshape([-1 if axis == axis_at else 1 for axis in range(len(dims))])
    return factor_of


def noise(stream_key, shape, scale, most, shards=(), kind=jnp.bfloat16):
    factor_of = levels(stream_key, shape, shards, -0.22, 0.18) if shards else 1.0
    result = jax.random.normal(stream_key, shape, jnp.float32) * scale * factor_of
    return jnp.minimum(jnp.maximum(result, -most), most).astype(kind)


def setup_inputs(seed: int = 0) -> dict:
    seeds = jax.random.split(jax.random.key(seed), 7)
    return {
        "ingest": noise(seeds[0], (N_SEQ * CAP, D), 1.0, 6.0, ((0, 128), (1, 4))),
        "ingest_count": draw_ingest_count(jax.random.fold_in(seeds[6], 71), 0),
        "doc_lengths": draw_doc_lengths(jax.random.fold_in(seeds[6], 71), 0),
        "in_weight": noise(seeds[3], (D, CH), D ** -0.5, 0.09375, ((0, 128), (1, 4))),
        "conv_weight": noise(seeds[4], (TAPS, CH), 0.5, 3.0, ((1, 4),), jnp.float32),
        "conv_bias": noise(seeds[5], (CH,), 0.5, 3.0, ((0, 4),), jnp.float32),
    }


def reference(ingest, ingest_count, doc_lengths, in_weight, conv_weight, conv_bias):
    counts = ingest_count
    offsets = jnp.cumsum(counts) - counts
    slots = jnp.arange(CAP, dtype=jnp.int32)
    target = offsets[:, None] + slots[None, :]
    target = jnp.where(slots[None, :] < counts[:, None], target, TOKENS).reshape(-1).astype(jnp.int32)
    stream = jnp.zeros((TOKENS, D), ingest.dtype).at[target].set(ingest, mode="drop")
    blocks = stream.reshape(N_SEQ, TOK_DEV, D)
    projected = lax.map(lambda block: jnp.dot(block, in_weight, preferred_element_type=jnp.float32).astype(jnp.bfloat16), blocks)
    values = projected.reshape(TOKENS, CH).astype(jnp.float32)
    starts = (jnp.cumsum(doc_lengths) - doc_lengths).astype(jnp.int32)
    places = jnp.arange(TOKENS, dtype=jnp.int32)
    doc_ids = (jnp.searchsorted(starts, places, side="right") - 1).astype(jnp.int32)
    total = jnp.zeros((TOKENS, CH), jnp.float32) + conv_bias[None, :]
    for lag in range(TAPS):
        earlier = jnp.pad(values, ((lag, 0), (0, 0)))[:TOKENS]
        earlier_ids = jnp.pad(doc_ids, (lag, 0), constant_values=-1)[:TOKENS]
        same = (earlier_ids == doc_ids).astype(jnp.float32)
        total = total + conv_weight[lag][None, :] * earlier * same[:, None]
    return jax.nn.silu(total).astype(jnp.bfloat16)
```

```python
import functools

import jax
import jax.numpy as jnp
from jax import lax
from jax.experimental import pallas as pl
from jax.experimental.pallas import tpu as pltpu
from jax.sharding import PartitionSpec as P

MESH = pl.DeviceIdType.MESH
F32 = jnp.float32
BF16 = jnp.bfloat16
NY, NX = 4, 4
PLANE = 2 * NY
LEAD = 16


def onehot(rows, columns, shift):
    q = lax.broadcasted_iota(jnp.int32, (rows, columns), 0)
    k = lax.broadcasted_iota(jnp.int32, (rows, columns), 1)
    return k - q == shift


def pick(mask):
    return jnp.where(mask, 1.0, 0.0).astype(BF16)


def dot(a, b):
    return jnp.dot(a, b, preferred_element_type=F32)


def names(nz):
    table, half = {}, nz // 2

    def add(*key):
        table[key] = len(table)

    for d in range(1, PLANE):
        add("c1", d)
    for d in range(1, nz):
        add("c2", d)
    add("pair")
    for h in range(2):
        add("tail", h)
        add("head", h)
        for r in range(4):
            add("xr", h, r)
            add("xl", h, r)
            add("xf", h, r)
    for d in range(1, NY):
        add("ya", d)
    for s in range(1, half + 1):
        for j in range(NY):
            add("ua", s, j)
            add("da", s, j)
        add("ub", s)
        add("db", s)
    for t in range(nz):
        add("yu", t)
        add("yd", t)
        add("yf", t)
        add("pass", t)
    return table


def kernel(nz, table, count_ref, lens_ref, taps_ref, bias_ref, ingest, weight, out,
           ing, tail_s, tail_r, head_r, wa, wb, feat, proj, keep, cnt1, cnt2,
           sel_t, sel_o, sel_b, sel_h, outv, lsem, ssem, rsem):
    half = nz // 2
    tokens = outv.shape[0]
    hrows = tokens // 2
    trows = hrows + LEAD
    unit = tokens // 4
    depth, ca = weight.shape[0], wa.shape[1]
    cb = wb.shape[1]
    hcols = feat.shape[2]
    pair_rows = 2 * depth
    plane_rows = PLANE * depth
    per_x = nz * plane_rows // NX

    s = lax.axis_index("seq")
    x = lax.axis_index("ch")
    core = lax.rem(s, 2)
    p = lax.rem(s, PLANE)
    y = p // 2
    z = s // PLANE
    count_devices = nz * PLANE

    def at(zz, yy, cc):
        return {"seq": (zz * NY + yy) * 2 + cc, "ch": x}

    def zof(d):
        return lax.rem(z + (d + 2 * nz), nz)

    def yof(d):
        return lax.rem(y + (d + 2 * NY), NY)

    def xof(d):
        return lax.rem(x + (d + 2 * NX), NX)

    right = {"seq": lax.rem(s + 1, count_devices), "ch": x}
    left = {"seq": lax.rem(s + count_devices - 1, count_devices), "ch": x}
    sibling = {"seq": s + 1 - 2 * core, "ch": x}
    far = {"seq": lax.rem(s + count_devices - 1 + 2 * core, count_devices), "ch": x}
    xright = {"seq": s, "ch": xof(1)}
    xleft = {"seq": s, "ch": xof(-1)}

    def blk(zz, yy):
        return pl.ds(pl.multiple_of((zz * NY + yy) * pair_rows, pair_rows), pair_rows)

    def plane(zz):
        return pl.ds(pl.multiple_of(zz * plane_rows, plane_rows), plane_rows)

    def rc(key, src, dst, device):
        i = table[key]
        return pltpu.make_async_remote_copy(
            src_ref=src, dst_ref=dst, send_sem=ssem.at[i], recv_sem=rsem.at[i],
            device_id=device, device_id_type=MESH)

    sent = {None: [], 0: [], 1: []}

    def send(who, make, *args):
        make(*args).start()
        sent[who].append((make, args))

    def c1(d):
        peer = lax.rem(p + d, PLANE)
        return rc(("c1", d), cnt1.at[0], cnt1.at[d], {"seq": z * PLANE + peer, "ch": x})

    def c2(d):
        return rc(("c2", d), cnt2.at[0], cnt2.at[d], {"seq": zof(d) * PLANE + p, "ch": x})

    mine = pl.ds(pl.multiple_of(s * depth, depth), depth)

    def pair_to0():
        return rc(("pair",), weight.at[:, 0:ca], wa.at[mine], sibling)

    def pair_to1():
        return rc(("pair",), weight.at[:, ca:], wb.at[mine], sibling)

    def tail(h):
        return rc(("tail", h), tail_s.at[h], tail_r.at[h], right)

    def head(h):
        return rc(("head", h), ingest.at[0:hrows, h * hcols:(h + 1) * hcols], head_r.at[h], left)

    def xrows(r):
        return pl.ds(0, LEAD + unit) if r == 0 else pl.ds(LEAD + r * unit, unit)

    def xcopy(kind, h, r, source, device):
        block = feat.at[source * 2 + h, xrows(r)]
        return rc((kind, h, r), block, block, device)

    def xr(h, r):
        return xcopy("xr", h, r, x, xright)

    def xl(h, r):
        return xcopy("xl", h, r, x, xleft)

    def xf(h, r):
        if r % 2 == 0:
            return xcopy("xf", h, r, xof(-1), xright)
        return xcopy("xf", h, r, xof(1), xleft)

    def ya(d):
        block = wa.at[blk(z, y)]
        return rc(("ya", d), block, block, at(z, yof(d), 0))

    def ua(st, j):
        block = wa.at[blk(zof(1 - st), yof(-j))]
        return rc(("ua", st, j), block, block, at(zof(1), y, 0))

    def da(st, j):
        block = wa.at[blk(zof(st - 1), yof(-j))]
        return rc(("da", st, j), block, block, at(zof(-1), y, 0))

    def part(zz, yy, piece):
        if piece is None:
            return blk(zz, yy)
        first = (zz * NY + yy) * pair_rows + piece * depth
        return pl.ds(pl.multiple_of(first, depth), depth)

    def ub(st):
        block = wb.at[part(zof(1 - st), y, 0 if st == half else None)]
        return rc(("ub", st), block, block, at(zof(1), y, 1))

    def db(st):
        block = wb.at[part(zof(st - 1), y, 1 if st == half else None)]
        return rc(("db", st), block, block, at(zof(-1), y, 1))

    def yu(t):
        block = wb.at[blk(zof(-t), y)]
        return rc(("yu", t), block, block, at(z, yof(1), 1))

    def yd(t):
        block = wb.at[blk(zof(-t), y)]
        return rc(("yd", t), block, block, at(z, yof(-1), 1))

    def yf(t):
        step = 1 if t % 2 == 0 else -1
        block = wb.at[blk(zof(-t), yof(-step))]
        return rc(("yf", t), block, block, at(z, yof(step), 1))

    def pass_a(t):
        block = wa.at[plane(zof(-t))]
        return rc(("pass", t), block, block, sibling)

    def pass_b(t):
        block = wb.at[plane(zof(-t))]
        return rc(("pass", t), block, block, sibling)

    def planes(st):
        return [st] if st in (0, half) else [st, nz - st]

    load = pltpu.make_async_copy(ingest, ing, lsem.at[0])
    load.start()

    def own_a():
        return pltpu.make_async_copy(weight.at[:, 0:ca], wa.at[mine], lsem.at[1])

    def own_b():
        return pltpu.make_async_copy(weight.at[:, ca:], wb.at[mine], lsem.at[1])

    @pl.when(core == 0)
    def _():
        own_a().start()

    @pl.when(core == 1)
    def _():
        own_b().start()

    barrier = pltpu.get_barrier_semaphore()
    friends = [{"seq": z * PLANE + lax.rem(p + d, PLANE), "ch": x} for d in range(1, PLANE)]
    friends += [{"seq": zof(d) * PLANE + p, "ch": x} for d in range(1, nz)]
    friends += [far, xright, xleft]
    for friend in friends:
        pl.semaphore_signal(barrier, inc=1, device_id=friend, device_id_type=MESH)

    count = count_ref[0]
    cnt1[0] = jnp.full(cnt1.shape[1:], count, jnp.int32)
    load.wait()
    tail_pick = pick(onehot(trows, ing.shape[0], count - trows))
    for h in range(2):
        tail_s[h] = dot(tail_pick, ing[:, h * hcols:(h + 1) * hcols]).astype(BF16)
    pl.semaphore_wait(barrier, len(friends))

    for d in range(1, PLANE):
        send(None, c1, d)

    @pl.when(core == 0)
    def _():
        send(0, pair_to1)

    @pl.when(core == 1)
    def _():
        send(1, pair_to0)

    send(None, tail, 0)
    send(None, head, 0)
    total = cnt1[0]
    inside = jnp.zeros_like(total)
    for d in range(1, PLANE):
        c1(d).wait_recv()
        total += cnt1[d]
        inside += jnp.where(lax.rem(p + PLANE - d, PLANE) < p, cnt1[d], 0)
    cnt2[0] = total
    for d in range(1, nz):
        send(None, c2, d)
    send(None, tail, 1)
    send(None, head, 1)

    @pl.when(core == 0)
    def _():
        own_a().wait()
        pair_to0().wait_recv()
        for d in range(1, NY):
            send(0, ya, d)
        send(0, ua, 1, 0)
        send(0, da, 1, 0)
        for j in range(1, NY):
            ya(j).wait_recv()
            if half > 1 or j < NY // 2:
                send(0, ua, 1, j)
            if half > 1 or j >= NY // 2:
                send(0, da, 1, j)
        send(0, pass_a, 0)

    @pl.when(core == 1)
    def _():
        own_b().wait()
        pair_to1().wait_recv()
        send(1, ub, 1)
        send(1, db, 1)
        send(1, yu, 0)
        send(1, yd, 0)

    for d in range(1, nz):
        c2(d).wait_recv()
        inside += jnp.where(lax.rem(z + nz - d, nz) < z, cnt2[d], 0)
    shift = s * tokens - inside[0:1, 0:1]
    top = pick(onehot(trows, trows + 2 * hrows, hrows + shift))
    sel_t[...] = top[:, :trows]
    sel_o[...] = top[:, trows:]
    slot = lax.broadcasted_iota(jnp.int32, (hrows, 3 * hrows), 1)
    sel_b[...] = pick(onehot(hrows, 3 * hrows, hrows + shift) & (slot < count))
    sel_h[...] = pick(onehot(hrows, hrows, hrows + shift - count))

    def assemble(h):
        tail(h).wait_recv()
        head(h).wait_recv()
        cols = slice(h * hcols, (h + 1) * hcols)
        spot = x * 2 + h
        feat[spot, 0:trows] = (
            dot(sel_t[...], tail_r[h]) + dot(sel_o[...], ing[0:2 * hrows, cols])).astype(BF16)
        feat[spot, trows:trows + hrows] = (
            dot(sel_b[...], ing[0:3 * hrows, cols]) + dot(sel_h[...], head_r[h])).astype(BF16)
        for r in range(4):
            send(None, xr, h, r)
            send(None, xl, h, r)

    def step_a(st):
        for j in range(NY):
            if st < half or j < NY // 2:
                ua(st, j).wait_recv()
            if st + 1 < half or (st + 1 == half and j < NY // 2):
                send(0, ua, st + 1, j)
            if st < half or j >= NY // 2:
                da(st, j).wait_recv()
            if st + 1 < half or (st + 1 == half and j >= NY // 2):
                send(0, da, st + 1, j)
        for t in planes(st):
            send(0, pass_a, t)

    def step_b(st):
        if st <= half:
            ub(st).wait_recv()
            if st < half:
                send(1, ub, st + 1)
            db(st).wait_recv()
            if st < half:
                send(1, db, st + 1)
            for t in planes(st):
                send(1, yu, t)
                send(1, yd, t)
        if 1 <= st <= half + 1:
            for t in planes(st - 1):
                yu(t).wait_recv()
                yd(t).wait_recv()
                send(1, yf, t)
        if 2 <= st <= half + 2:
            for t in planes(st - 2):
                yf(t).wait_recv()
                send(1, pass_b, t)

    units = [(h, r) for h in range(2) for r in range(4)]

    def xforward(h, r):
        xr(h, r).wait_recv()
        xl(h, r).wait_recv()
        send(None, xf, h, r)

    assemble(0)
    assemble(1)
    waiting = list(units)
    for st in range(1, half + 1):
        @pl.when(core == 0)
        def _():
            step_a(st)

        @pl.when(core == 1)
        def _():
            step_b(st)

        if st == 1:
            row = lax.broadcasted_iota(jnp.int32, (128, 128), 0)
            col = lax.broadcasted_iota(jnp.int32, (128, 128), 1)
            lens = lens_ref[...].astype(F32)
            lens_col = jnp.sum(jnp.where(row == col, lens, 0.0), axis=1, keepdims=True)
            starts = jnp.sum(jnp.where(row < col, lens_col, 0.0), axis=0, keepdims=True)
            places = (s * tokens + lax.broadcasted_iota(jnp.int32, (tokens, 128), 0)).astype(F32)
            since = places - starts
            age = jnp.min(jnp.where(since >= 0.0, since, 1e9), axis=1, keepdims=True)
            for lag in range(1, 4):
                keep[lag - 1] = jnp.broadcast_to(jnp.where(age >= lag, 1.0, 0.0), (tokens, 128))
        if st >= 2 and waiting:
            xforward(*waiting.pop(0))
    while waiting:
        xforward(*waiting.pop(0))

    @pl.when(core == 0)
    def _():
        for t in range(nz):
            pass_b(t).wait_recv()

    @pl.when(core == 1)
    def _():
        step_b(half + 1)
        step_b(half + 2)
        for t in range(nz):
            pass_a(t).wait_recv()

    def project(first, rows, rels, fresh, last):
        def columns(w, base, width, number):
            @pl.loop(0, number)
            def _(n):
                from_ = pl.ds(pl.multiple_of(n * width, width), width)
                to = pl.ds(pl.multiple_of(base + n * width, 128), width)
                value = None if fresh else proj[first:first + rows, to]
                for rel in rels:
                    source = xof(rel)
                    for h in range(2):
                        deep = pl.ds(pl.multiple_of(source * per_x + h * hcols, hcols), hcols)
                        term = dot(feat[source * 2 + h, first:first + rows], w[deep, from_])
                        value = term if value is None else value + term
                if last:
                    value = value.astype(BF16).astype(F32)
                proj[first:first + rows, to] = value

        width = min(256, ca)
        columns(wa, 0, width, ca // width)
        columns(wb, ca, width, cb // width)

    def activate(first, rows):
        block = min(64, rows)

        @pl.loop(0, rows // block)
        def _(n):
            base = pl.multiple_of(first + n * block, block)
            here = pl.ds(base, block)
            for c in range((ca + cb) // 128):
                cols = slice(c * 128, (c + 1) * 128)
                window = proj[pl.ds(pl.multiple_of(base + LEAD - 8, 8), block + 8), cols]
                value = bias_ref[:, cols] + taps_ref[0:1, cols] * window[8:]
                for lag in range(1, 4):
                    value += taps_ref[lag:lag + 1, cols] * window[8 - lag:8 - lag + block] * keep[lag - 1, here]
                outv[here, cols] = (value / (1.0 + jnp.exp(-value))).astype(BF16)

        rows_ = pl.ds(first, rows)
        copy = pltpu.make_async_copy(outv.at[rows_], out.at[rows_], lsem.at[2 + first // hrows])
        copy.start()
        return copy

    for h in range(2):
        for r in range(2):
            xf(h, r).wait_recv()
    project(0, trows, (0, -1, 1, 2), True, True)
    copy0 = activate(0, hrows)
    project(trows, hrows, (0, -1, 1), True, False)
    for h in range(2):
        for r in range(2, 4):
            xf(h, r).wait_recv()
    project(trows, hrows, (2,), False, True)
    copy1 = activate(hrows, hrows)

    for make, args in sent[None]:
        make(*args).wait_send()

    @pl.when(core == 0)
    def _():
        for make, args in sent[0]:
            make(*args).wait_send()

    @pl.when(core == 1)
    def _():
        for make, args in sent[1]:
            make(*args).wait_send()

    copy0.wait()
    copy1.wait()


def body(ingest, ingest_count, doc_lengths, in_weight, conv_weight, conv_bias, interpret=False):
    nz = lax.axis_size("seq") // PLANE
    table = names(nz)
    tokens = ingest.shape[0] // 2
    hrows, trows = tokens // 2, tokens // 2 + LEAD
    depth, channels = in_weight.shape
    features = ingest.shape[1]
    hcols = features // 2
    ca = channels * 2 // 5 // 128 * 128
    cb = channels - ca
    total_depth = nz * PLANE * depth
    vmem = pl.BlockSpec(memory_space=pltpu.VMEM)
    hbm = pl.BlockSpec(memory_space=pl.ANY)
    flops = 2 * tokens * total_depth * channels
    return pl.pallas_call(
        functools.partial(kernel, nz, table),
        out_shape=jax.ShapeDtypeStruct((tokens, channels), BF16),
        in_specs=[pl.BlockSpec(memory_space=pltpu.SMEM), vmem, vmem, vmem, hbm, hbm],
        out_specs=hbm,
        scratch_shapes=[
            pltpu.VMEM(ingest.shape, BF16),
            pltpu.VMEM((2, trows, hcols), BF16),
            pltpu.VMEM((2, trows, hcols), BF16),
            pltpu.VMEM((2, hrows, hcols), BF16),
            pltpu.VMEM((total_depth, ca), BF16),
            pltpu.VMEM((total_depth, cb), BF16),
            pltpu.VMEM((2 * NX, LEAD + tokens, hcols), BF16),
            pltpu.VMEM((LEAD + tokens, channels), F32),
            pltpu.VMEM((3, tokens, 128), F32),
            pltpu.VMEM((PLANE, 8, 128), jnp.int32),
            pltpu.VMEM((nz, 8, 128), jnp.int32),
            pltpu.VMEM((trows, trows), BF16),
            pltpu.VMEM((trows, 2 * hrows), BF16),
            pltpu.VMEM((hrows, 3 * hrows), BF16),
            pltpu.VMEM((hrows, hrows), BF16),
            pltpu.VMEM((tokens, channels), BF16),
            pltpu.SemaphoreType.DMA((4,)),
            pltpu.SemaphoreType.DMA((len(table),)),
            pltpu.SemaphoreType.DMA((len(table),)),
        ],
        compiler_params=pltpu.CompilerParams(
            collective_id=0, has_side_effects=True, vmem_limit_bytes=48 * 1024 * 1024),
        cost_estimate=pl.CostEstimate(flops=flops, bytes_accessed=20 << 20, transcendentals=tokens * channels),
    )(ingest_count, doc_lengths.reshape(1, -1), conv_weight, conv_bias.reshape(1, -1), ingest, in_weight)


def solution(mesh):
    placed = (P("seq", "ch"), P("seq"), P(), P("seq", "ch"), P(None, "ch"), P("ch"))
    return jax.shard_map(
        body, mesh=mesh, in_specs=placed, out_specs=P("seq", "ch"), check_vma=False
    )
```

```python
import functools

import jax
import jax.numpy as jnp
from jax import lax
from jax.experimental import pallas as pl
from jax.experimental.pallas import tpu as pltpu
from jax.sharding import PartitionSpec as P

MESH = pl.DeviceIdType.MESH
F32 = jnp.float32
BF16 = jnp.bfloat16
NY, NX = 4, 4
PLANE = 2 * NY
LEAD = 16


def onehot(rows, columns, shift):
    q = lax.broadcasted_iota(jnp.int32, (rows, columns), 0)
    k = lax.broadcasted_iota(jnp.int32, (rows, columns), 1)
    return k - q == shift


def pick(mask):
    return jnp.where(mask, 1.0, 0.0).astype(BF16)


def dot(a, b):
    return jnp.dot(a, b, preferred_element_type=F32)


def names(nz):
    table, half = {}, nz // 2

    def add(*key):
        table[key] = len(table)

    for d in range(1, PLANE):
        add("c1", d)
    for d in range(1, half):
        add("c2", d)
    add("pair")
    for h in range(2):
        add("tail", h)
        add("head", h)
        for r in range(4):
            add("xr", h, r)
            add("xl", h, r)
            add("xf", h, r)
    for d in range(1, NY):
        add("ya", d)
    for s in range(1, half + 1):
        for j in range(NY):
            add("ua", s, j)
            add("da", s, j)
        for piece in range(2):
            add("ub", s, piece)
            add("db", s, piece)
    for t in range(nz):
        add("yu", t)
        add("yd", t)
        add("yf", t)
        add("pass", t)
    return table


def kernel(nz, table, rows_total, count_hbm, lens_hbm, taps_hbm, bias_hbm, ingest, weight, out,
           count_ref, lens_ref, taps_ref, bias_ref, ing, tail_s, tail_r, head_r, wa, wb, feat, proj, keep, cnt1, cnt2,
           sel_t, sel_o, sel_b, sel_h, outv, lsem, ssem, rsem):
    half = nz // 2
    tokens = outv.shape[0]
    hrows = tokens // 2
    trows = hrows + LEAD
    unit = tokens // 4
    depth, ca = weight.shape[0], wa.shape[1]
    cb = wb.shape[1]
    hcols = feat.shape[2]
    pair_rows = 2 * depth
    plane_rows = PLANE * depth
    per_x = nz * plane_rows // NX

    s = lax.axis_index("seq")
    x = lax.axis_index("ch")
    core = lax.rem(s, 2)
    p = lax.rem(s, PLANE)
    y = p // 2
    z = s // PLANE
    count_devices = nz * PLANE

    def at(zz, yy, cc):
        return {"seq": (zz * NY + yy) * 2 + cc, "ch": x}

    def zof(d):
        return lax.rem(z + (d + 2 * nz), nz)

    zlow = lax.rem(z, half)

    def zpeer(d):
        return z - zlow + lax.rem(zlow + d, half)

    def yof(d):
        return lax.rem(y + (d + 2 * NY), NY)

    def xof(d):
        return lax.rem(x + (d + 2 * NX), NX)

    right = {"seq": lax.rem(s + 1, count_devices), "ch": x}
    left = {"seq": lax.rem(s + count_devices - 1, count_devices), "ch": x}
    sibling = {"seq": s + 1 - 2 * core, "ch": x}
    far = {"seq": lax.rem(s + count_devices - 1 + 2 * core, count_devices), "ch": x}
    xright = {"seq": s, "ch": xof(1)}
    xleft = {"seq": s, "ch": xof(-1)}

    def blk(zz, yy):
        return pl.ds(pl.multiple_of((zz * NY + yy) * pair_rows, pair_rows), pair_rows)

    def plane(zz):
        return pl.ds(pl.multiple_of(zz * plane_rows, plane_rows), plane_rows)

    def rc(key, src, dst, device):
        i = table[key]
        return pltpu.make_async_remote_copy(
            src_ref=src, dst_ref=dst, send_sem=ssem.at[i], recv_sem=rsem.at[i],
            device_id=device, device_id_type=MESH)

    sent = {None: [], 0: [], 1: []}

    def send(who, make, *args):
        make(*args).start()
        sent[who].append((make, args))

    def c1(d):
        peer = lax.rem(p + d, PLANE)
        return rc(("c1", d), cnt1.at[0], cnt1.at[d], {"seq": z * PLANE + peer, "ch": x})

    def c2(d):
        return rc(("c2", d), cnt2.at[0], cnt2.at[d], {"seq": zpeer(d) * PLANE + p, "ch": x})

    mine = pl.ds(pl.multiple_of(s * depth, depth), depth)

    def pair_to0():
        return rc(("pair",), weight.at[:, 0:ca], wa.at[mine], sibling)

    def pair_to1():
        return rc(("pair",), weight.at[:, ca:], wb.at[mine], sibling)

    def tail(h):
        return rc(("tail", h), tail_s.at[h], tail_r.at[h], right)

    def head(h):
        return rc(("head", h), ingest.at[0:hrows, h * hcols:(h + 1) * hcols], head_r.at[h], left)

    def xrows(r):
        return pl.ds(0, LEAD + unit) if r == 0 else pl.ds(LEAD + r * unit, unit)

    def xcopy(kind, h, r, source, device):
        block = feat.at[source * 2 + h, xrows(r)]
        return rc((kind, h, r), block, block, device)

    def xr(h, r):
        return xcopy("xr", h, r, x, xright)

    def xl(h, r):
        return xcopy("xl", h, r, x, xleft)

    def xf(h, r):
        if r % 2 == 0:
            return xcopy("xf", h, r, xof(-1), xright)
        return xcopy("xf", h, r, xof(1), xleft)

    def ya(d):
        block = wa.at[blk(z, y)]
        return rc(("ya", d), block, block, at(z, yof(d), 0))

    def ua(st, j):
        block = wa.at[blk(zof(1 - st), yof(-j))]
        return rc(("ua", st, j), block, block, at(zof(1), y, 0))

    def da(st, j):
        block = wa.at[blk(zof(st - 1), yof(-j))]
        return rc(("da", st, j), block, block, at(zof(-1), y, 0))

    def part(zz, yy, piece):
        first = (zz * NY + yy) * pair_rows + piece * depth
        return pl.ds(pl.multiple_of(first, depth), depth)

    def ub(st, piece):
        block = wb.at[part(zof(1 - st), y, piece)]
        return rc(("ub", st, piece), block, block, at(zof(1), y, 1))

    def db(st, piece):
        block = wb.at[part(zof(st - 1), y, piece)]
        return rc(("db", st, piece), block, block, at(zof(-1), y, 1))

    def goes(way, st, piece):
        return st < half or (st == half and piece == way)

    def yu(t):
        block = wb.at[blk(zof(-t), y)]
        return rc(("yu", t), block, block, at(z, yof(1), 1))

    def yd(t):
        block = wb.at[blk(zof(-t), y)]
        return rc(("yd", t), block, block, at(z, yof(-1), 1))

    def yf(t):
        step = 1 if t % 2 == 0 else -1
        block = wb.at[blk(zof(-t), yof(-step))]
        return rc(("yf", t), block, block, at(z, yof(step), 1))

    def pass_a(t):
        block = wa.at[plane(zof(-t))]
        return rc(("pass", t), block, block, sibling)

    def pass_b(t):
        block = wb.at[plane(zof(-t))]
        return rc(("pass", t), block, block, sibling)

    def planes(st):
        return [st] if st in (0, half) else [st, nz - st]

    load = pltpu.make_async_copy(ingest, ing, lsem.at[0])
    small = [pltpu.make_async_copy(a, b, lsem.at[4 + i]) for i, (a, b) in enumerate(
        ((count_hbm, count_ref), (lens_hbm, lens_ref), (taps_hbm, taps_ref), (bias_hbm, bias_ref)))]
    small[0].start()
    load.start()

    def own_a():
        return pltpu.make_async_copy(weight.at[:, 0:ca], wa.at[mine], lsem.at[1])

    def own_b():
        return pltpu.make_async_copy(weight.at[:, ca:], wb.at[mine], lsem.at[1])

    @pl.when(core == 0)
    def _():
        own_a().start()

    @pl.when(core == 1)
    def _():
        own_b().start()

    barrier = pltpu.get_barrier_semaphore()
    friends = [{"seq": zpeer(d) * PLANE + p, "ch": x} for d in range(1, half)]
    friends += [at(zof(1), y, core), at(zof(-1), y, core), far, xright, xleft]
    friends += [{"seq": z * PLANE + lax.rem(p + d, PLANE), "ch": x} for d in range(1, PLANE)]
    for friend in friends:
        pl.semaphore_signal(barrier, inc=1, device_id=friend, device_id_type=MESH)
    for copy in small[1:]:
        copy.start()
    small[0].wait()
    count = count_ref[0]
    cnt1[0] = jnp.full(cnt1.shape[1:], count, jnp.int32)
    pl.semaphore_wait(barrier, len(friends))

    for d in range(1, PLANE):
        send(None, c1, d)

    @pl.when(core == 0)
    def _():
        send(0, pair_to1)

    @pl.when(core == 1)
    def _():
        send(1, pair_to0)

    send(None, head, 0)
    load.wait()
    tail_pick = pick(onehot(trows, ing.shape[0], count - trows))
    tail_s[0] = dot(tail_pick, ing[:, 0:hcols]).astype(BF16)
    send(None, tail, 0)
    total = cnt1[0]
    inside = jnp.zeros_like(total)
    for d in range(1, PLANE):
        c1(d).wait_recv()
        total += cnt1[d]
        inside += jnp.where(lax.rem(p + PLANE - d, PLANE) < p, cnt1[d], 0)
    cnt2[0] = total
    for d in range(1, half):
        send(None, c2, d)

    @pl.when(core == 0)
    def _():
        own_a().wait()
        pair_to0().wait_recv()
        send(0, ua, 1, 0)
        send(0, da, 1, 0)
        for d in range(1, NY):
            send(0, ya, d)

    @pl.when(core == 1)
    def _():
        own_b().wait()
        pair_to1().wait_recv()
        for piece in range(2):
            for way, ring in enumerate((ub, db)):
                if goes(way, 1, piece):
                    send(1, ring, 1, piece)
        send(1, yu, 0)
        send(1, yd, 0)

    tail_s[1] = dot(tail_pick, ing[:, hcols:]).astype(BF16)
    send(None, head, 1)
    send(None, tail, 1)

    group = cnt2[0]
    for d in range(1, half):
        c2(d).wait_recv()
        group += cnt2[d]
        inside += jnp.where(lax.rem(zlow + half - d, half) < zlow, cnt2[d], 0)
    inside += jnp.where(z >= half, rows_total - group, 0)
    shift = s * tokens - inside[0:1, 0:1]
    top = pick(onehot(trows, trows + 2 * hrows, hrows + shift))
    sel_t[...] = top[:, :trows]
    sel_o[...] = top[:, trows:]
    slot = lax.broadcasted_iota(jnp.int32, (hrows, 3 * hrows), 1)
    sel_b[...] = pick(onehot(hrows, 3 * hrows, hrows + shift) & (slot < count))
    sel_h[...] = pick(onehot(hrows, hrows, hrows + shift - count))

    def assemble(h):
        tail(h).wait_recv()
        head(h).wait_recv()
        cols = slice(h * hcols, (h + 1) * hcols)
        spot = x * 2 + h
        feat[spot, 0:trows] = (
            dot(sel_t[...], tail_r[h]) + dot(sel_o[...], ing[0:2 * hrows, cols])).astype(BF16)
        feat[spot, trows:trows + hrows] = (
            dot(sel_b[...], ing[0:3 * hrows, cols]) + dot(sel_h[...], head_r[h])).astype(BF16)
        for r in range(4):
            send(None, xr, h, r)
            send(None, xl, h, r)

    def step_a(st):
        if st == 0:
            for j in range(1, NY):
                ya(j).wait_recv()
                if half > 1 or j < NY // 2:
                    send(0, ua, 1, j)
                if half > 1 or j >= NY // 2:
                    send(0, da, 1, j)
            send(0, pass_a, 0)
            return
        for j in range(NY):
            if st < half or j < NY // 2:
                ua(st, j).wait_recv()
            if st + 1 < half or (st + 1 == half and j < NY // 2):
                send(0, ua, st + 1, j)
            if st < half or j >= NY // 2:
                da(st, j).wait_recv()
            if st + 1 < half or (st + 1 == half and j >= NY // 2):
                send(0, da, st + 1, j)
        for t in planes(st):
            send(0, pass_a, t)

    def step_b(st):
        if st <= half:
            for piece in range(2):
                for way, ring in enumerate((ub, db)):
                    if goes(way, st, piece):
                        ring(st, piece).wait_recv()
                    if goes(way, st + 1, piece):
                        send(1, ring, st + 1, piece)
            for t in planes(st):
                send(1, yu, t)
                send(1, yd, t)
        if 2 <= st <= half + 2:
            for t in planes(st - 2):
                yu(t).wait_recv()
                yd(t).wait_recv()
                send(1, yf, t)
        if 3 <= st <= half + 3:
            for t in planes(st - 3):
                yf(t).wait_recv()
                send(1, pass_b, t)

    units = [(h, r) for h in range(2) for r in range(4)]

    def xforward(h, r):
        xr(h, r).wait_recv()
        xl(h, r).wait_recv()
        send(None, xf, h, r)

    waiting = list(units)

    @pl.when(core == 0)
    def _():
        step_a(0)

    for st in range(1, half + 1):
        if st <= 2:
            assemble(st - 1)

        @pl.when(core == 0)
        def _():
            step_a(st)

        @pl.when(core == 1)
        def _():
            step_b(st)

        if st == 3 or half < 3 and st == half:
            for copy in small[1:]:
                copy.wait()
            row = lax.broadcasted_iota(jnp.int32, (128, 128), 0)
            col = lax.broadcasted_iota(jnp.int32, (128, 128), 1)
            lens = lens_ref[...].astype(F32)
            lens_col = jnp.sum(jnp.where(row == col, lens, 0.0), axis=1, keepdims=True)
            starts = jnp.sum(jnp.where(row < col, lens_col, 0.0), axis=0, keepdims=True)
            places = (s * tokens + lax.broadcasted_iota(jnp.int32, (tokens, 128), 0)).astype(F32)
            since = places - starts
            age = jnp.min(jnp.where(since >= 0.0, since, 1e9), axis=1, keepdims=True)
            for lag in range(1, 4):
                keep[lag - 1] = jnp.broadcast_to(jnp.where(age >= lag, 1.0, 0.0), (tokens, 128))
        if st >= 2 and waiting:
            xforward(*waiting.pop(0))
    while waiting:
        xforward(*waiting.pop(0))

    @pl.when(core == 0)
    def _():
        for t in range(nz):
            pass_b(t).wait_recv()

    @pl.when(core == 1)
    def _():
        step_b(half + 1)
        step_b(half + 2)
        step_b(half + 3)
        for t in range(nz):
            pass_a(t).wait_recv()

    def project(first, rows, rels, fresh, last):
        def columns(w, base, width, number):
            @pl.loop(0, number)
            def _(n):
                from_ = pl.ds(pl.multiple_of(n * width, width), width)
                to = pl.ds(pl.multiple_of(base + n * width, 128), width)
                value = None if fresh else proj[first:first + rows, to]
                for rel in rels:
                    source = xof(rel)
                    for h in range(2):
                        deep = pl.ds(pl.multiple_of(source * per_x + h * hcols, hcols), hcols)
                        term = dot(feat[source * 2 + h, first:first + rows], w[deep, from_])
                        value = term if value is None else value + term
                if last:
                    value = value.astype(BF16).astype(F32)
                proj[first:first + rows, to] = value

        width = min(256, ca)
        columns(wa, 0, width, ca // width)
        columns(wb, ca, width, cb // width)

    def activate(first, rows):
        block = min(64, rows)

        @pl.loop(0, rows // block)
        def _(n):
            base = pl.multiple_of(first + n * block, block)
            here = pl.ds(base, block)
            for c in range((ca + cb) // 128):
                cols = slice(c * 128, (c + 1) * 128)
                window = proj[pl.ds(pl.multiple_of(base + LEAD - 8, 8), block + 8), cols]
                value = bias_ref[cols].reshape(1, 128) + taps_ref[0:1, cols] * window[8:]
                for lag in range(1, 4):
                    value += taps_ref[lag:lag + 1, cols] * window[8 - lag:8 - lag + block] * keep[lag - 1, here]
                outv[here, cols] = (value / (1.0 + jnp.exp(-value))).astype(BF16)

        rows_ = pl.ds(first, rows)
        copy = pltpu.make_async_copy(outv.at[rows_], out.at[rows_], lsem.at[2 + first // hrows])
        copy.start()
        return copy

    for h in range(2):
        for r in range(2):
            xf(h, r).wait_recv()
    project(0, trows, (0, -1, 1, 2), True, True)
    copy0 = activate(0, hrows)
    project(trows, hrows, (0, -1, 1), True, False)
    for h in range(2):
        for r in range(2, 4):
            xf(h, r).wait_recv()
    project(trows, hrows, (2,), False, True)
    copy1 = activate(hrows, hrows)

    for make, args in sent[None]:
        make(*args).wait_send()

    @pl.when(core == 0)
    def _():
        for make, args in sent[0]:
            make(*args).wait_send()

    @pl.when(core == 1)
    def _():
        for make, args in sent[1]:
            make(*args).wait_send()

    copy0.wait()
    copy1.wait()


def body(ingest, ingest_count, doc_lengths, in_weight, conv_weight, conv_bias):
    nz = lax.axis_size("seq") // PLANE
    table = names(nz)
    tokens = ingest.shape[0] // 2
    hrows, trows = tokens // 2, tokens // 2 + LEAD
    depth, channels = in_weight.shape
    features = ingest.shape[1]
    hcols = features // 2
    ca = channels * 2 // 5 // 128 * 128
    cb = channels - ca
    total_depth = nz * PLANE * depth
    hbm = pl.BlockSpec(memory_space=pltpu.HBM)
    flops = 2 * tokens * total_depth * channels
    return pl.pallas_call(
        functools.partial(kernel, nz, table, nz * PLANE * tokens),
        out_shape=jax.ShapeDtypeStruct((tokens, channels), BF16),
        in_specs=[hbm] * 6,
        out_specs=hbm,
        scratch_shapes=[
            pltpu.SMEM((1,), jnp.int32),
            pltpu.VMEM((1, 128), jnp.int32),
            pltpu.VMEM(conv_weight.shape, F32),
            pltpu.VMEM(conv_bias.shape, F32),
            pltpu.VMEM(ingest.shape, BF16),
            pltpu.VMEM((2, trows, hcols), BF16),
            pltpu.VMEM((2, trows, hcols), BF16),
            pltpu.VMEM((2, hrows, hcols), BF16),
            pltpu.VMEM((total_depth, ca), BF16),
            pltpu.VMEM((total_depth, cb), BF16),
            pltpu.VMEM((2 * NX, LEAD + tokens, hcols), BF16),
            pltpu.VMEM((LEAD + tokens, channels), F32),
            pltpu.VMEM((3, tokens, 128), F32),
            pltpu.VMEM((PLANE, 8, 128), jnp.int32),
            pltpu.VMEM((nz // 2, 8, 128), jnp.int32),
            pltpu.VMEM((trows, trows), BF16),
            pltpu.VMEM((trows, 2 * hrows), BF16),
            pltpu.VMEM((hrows, 3 * hrows), BF16),
            pltpu.VMEM((hrows, hrows), BF16),
            pltpu.VMEM((tokens, channels), BF16),
            pltpu.SemaphoreType.DMA((8,)),
            pltpu.SemaphoreType.DMA((len(table),)),
            pltpu.SemaphoreType.DMA((len(table),)),
        ],
        compiler_params=pltpu.CompilerParams(
            collective_id=0, has_side_effects=True, vmem_limit_bytes=60 * 1024 * 1024),
        cost_estimate=pl.CostEstimate(flops=flops, bytes_accessed=20 << 20, transcendentals=tokens * channels),
    )(ingest_count, doc_lengths.reshape(1, -1), conv_weight, conv_bias, ingest, in_weight)


def solution(mesh):
    placed = (P("seq", "ch"), P("seq"), P(), P("seq", "ch"), P(None, "ch"), P("ch"))
    return jax.shard_map(
        body, mesh=mesh, in_specs=placed, out_specs=P("seq", "ch"), check_vma=False
    )
```

```python
import functools

import jax
import jax.numpy as jnp
from jax import lax
from jax.experimental import pallas as pl
from jax.experimental.pallas import tpu as pltpu
from jax.sharding import PartitionSpec as P

MESH = pl.DeviceIdType.MESH
F32 = jnp.float32
BF16 = jnp.bfloat16
NY, NX = 4, 4
PLANE = 2 * NY
LEAD = 16


def onehot(rows, columns, shift):
    q = lax.broadcasted_iota(jnp.int32, (rows, columns), 0)
    k = lax.broadcasted_iota(jnp.int32, (rows, columns), 1)
    return k - q == shift


def pick(mask):
    return jnp.where(mask, 1.0, 0.0).astype(BF16)


def dot(a, b):
    return jnp.dot(a, b, preferred_element_type=F32)


def names(nz):
    table, half = {}, nz // 2

    def add(*key):
        table[key] = len(table)

    for d in range(1, PLANE):
        add("c1", d)
    for d in range(1, half):
        add("c2", d)
    add("pair")
    for h in range(2):
        add("tail", h)
        add("head", h)
        for r in range(4):
            add("xr", h, r)
            add("xl", h, r)
            add("xf", h, r)
    for d in range(1, NY):
        add("ya", d)
    for s in range(1, half + 1):
        for j in range(NY):
            add("ua", s, j)
            add("da", s, j)
        for piece in range(2):
            add("ub", s, piece)
            add("db", s, piece)
    for t in range(nz):
        add("yu", t)
        add("yd", t)
        add("yf", t)
        add("pass", t)
    return table


def kernel(nz, table, rows_total, count_hbm, lens_hbm, taps_hbm, bias_hbm, ingest, weight, out,
           count_ref, lens_ref, taps_ref, bias_ref, ing, tail_s, tail_r, head_r, wa, wb, feat, proj, keep, cnt1, cnt2,
           sel_t, sel_o, sel_b, sel_h, outv, lsem, ssem, rsem):
    half = nz // 2
    tokens = outv.shape[0]
    hrows = tokens // 2
    trows = hrows + LEAD
    unit = tokens // 4
    depth, ca = weight.shape[0], wa.shape[1]
    cb = wb.shape[1]
    hcols = feat.shape[2]
    pair_rows = 2 * depth
    plane_rows = PLANE * depth
    per_x = nz * plane_rows // NX

    s = lax.axis_index("seq")
    x = lax.axis_index("ch")
    core = lax.rem(s, 2)
    p = lax.rem(s, PLANE)
    y = p // 2
    z = s // PLANE
    count_devices = nz * PLANE

    def at(zz, yy, cc):
        return {"seq": (zz * NY + yy) * 2 + cc, "ch": x}

    def zof(d):
        return lax.rem(z + (d + 2 * nz), nz)

    zlow = lax.rem(z, half)

    def zpeer(d):
        return z - zlow + lax.rem(zlow + d, half)

    def yof(d):
        return lax.rem(y + (d + 2 * NY), NY)

    def xof(d):
        return lax.rem(x + (d + 2 * NX), NX)

    right = {"seq": lax.rem(s + 1, count_devices), "ch": x}
    left = {"seq": lax.rem(s + count_devices - 1, count_devices), "ch": x}
    sibling = {"seq": s + 1 - 2 * core, "ch": x}
    far = {"seq": lax.rem(s + count_devices - 1 + 2 * core, count_devices), "ch": x}
    xright = {"seq": s, "ch": xof(1)}
    xleft = {"seq": s, "ch": xof(-1)}

    def blk(zz, yy):
        return pl.ds(pl.multiple_of((zz * NY + yy) * pair_rows, pair_rows), pair_rows)

    def plane(zz):
        return pl.ds(pl.multiple_of(zz * plane_rows, plane_rows), plane_rows)

    def rc(key, src, dst, device):
        i = table[key]
        return pltpu.make_async_remote_copy(
            src_ref=src, dst_ref=dst, send_sem=ssem.at[i], recv_sem=rsem.at[i],
            device_id=device, device_id_type=MESH)

    sent = {None: [], 0: [], 1: []}

    def send(who, make, *args):
        make(*args).start()
        sent[who].append((make, args))

    def c1(d):
        peer = lax.rem(p + d, PLANE)
        return rc(("c1", d), cnt1.at[0], cnt1.at[d], {"seq": z * PLANE + peer, "ch": x})

    def c2(d):
        return rc(("c2", d), cnt2.at[0], cnt2.at[d], {"seq": zpeer(d) * PLANE + p, "ch": x})

    mine = pl.ds(pl.multiple_of(s * depth, depth), depth)

    def pair_to0():
        return rc(("pair",), weight.at[:, 0:ca], wa.at[mine], sibling)

    def pair_to1():
        return rc(("pair",), weight.at[:, ca:], wb.at[mine], sibling)

    def tail(h):
        return rc(("tail", h), tail_s.at[h], tail_r.at[h], right)

    def head(h):
        return rc(("head", h), ingest.at[0:hrows, h * hcols:(h + 1) * hcols], head_r.at[h], left)

    def xrows(r):
        return pl.ds(0, LEAD + unit) if r == 0 else pl.ds(LEAD + r * unit, unit)

    def xcopy(kind, h, r, source, device):
        block = feat.at[source * 2 + h, xrows(r)]
        return rc((kind, h, r), block, block, device)

    def xr(h, r):
        return xcopy("xr", h, r, x, xright)

    def xl(h, r):
        return xcopy("xl", h, r, x, xleft)

    def xf(h, r):
        if r % 2 == 0:
            return xcopy("xf", h, r, xof(-1), xright)
        return xcopy("xf", h, r, xof(1), xleft)

    def ya(d):
        block = wa.at[blk(z, y)]
        return rc(("ya", d), block, block, at(z, yof(d), 0))

    def ua(st, j):
        block = wa.at[blk(zof(1 - st), yof(-j))]
        return rc(("ua", st, j), block, block, at(zof(1), y, 0))

    def da(st, j):
        block = wa.at[blk(zof(st - 1), yof(-j))]
        return rc(("da", st, j), block, block, at(zof(-1), y, 0))

    def part(zz, yy, piece):
        first = (zz * NY + yy) * pair_rows + piece * depth
        return pl.ds(pl.multiple_of(first, depth), depth)

    def ub(st, piece):
        block = wb.at[part(zof(1 - st), y, piece)]
        return rc(("ub", st, piece), block, block, at(zof(1), y, 1))

    def db(st, piece):
        block = wb.at[part(zof(st - 1), y, piece)]
        return rc(("db", st, piece), block, block, at(zof(-1), y, 1))

    def goes(way, st, piece):
        return st < half or (st == half and piece == way)

    def yu(t):
        block = wb.at[blk(zof(-t), y)]
        return rc(("yu", t), block, block, at(z, yof(1), 1))

    def yd(t):
        block = wb.at[blk(zof(-t), y)]
        return rc(("yd", t), block, block, at(z, yof(-1), 1))

    def yf(t):
        step = 1 if t % 2 == 0 else -1
        block = wb.at[blk(zof(-t), yof(-step))]
        return rc(("yf", t), block, block, at(z, yof(step), 1))

    def pass_a(t):
        block = wa.at[plane(zof(-t))]
        return rc(("pass", t), block, block, sibling)

    def pass_b(t):
        block = wb.at[plane(zof(-t))]
        return rc(("pass", t), block, block, sibling)

    def planes(st):
        return [st] if st in (0, half) else [st, nz - st]

    load = pltpu.make_async_copy(ingest, ing, lsem.at[0])
    small = [pltpu.make_async_copy(a, b, lsem.at[4 + i]) for i, (a, b) in enumerate(
        ((count_hbm, count_ref), (lens_hbm, lens_ref), (taps_hbm, taps_ref), (bias_hbm, bias_ref)))]
    small[0].start()
    load.start()

    def own_a():
        return pltpu.make_async_copy(weight.at[:, 0:ca], wa.at[mine], lsem.at[1])

    def own_b():
        return pltpu.make_async_copy(weight.at[:, ca:], wb.at[mine], lsem.at[1])

    @pl.when(core == 0)
    def _():
        own_a().start()

    @pl.when(core == 1)
    def _():
        own_b().start()

    barrier = pltpu.get_barrier_semaphore()
    friends = [{"seq": zpeer(d) * PLANE + p, "ch": x} for d in range(1, half)]
    friends += [at(zof(1), y, core), at(zof(-1), y, core), far, xright, xleft]
    friends += [{"seq": z * PLANE + lax.rem(p + d, PLANE), "ch": x} for d in range(1, PLANE)]
    for friend in friends:
        pl.semaphore_signal(barrier, inc=1, device_id=friend, device_id_type=MESH)
    for copy in small[1:]:
        copy.start()
    small[0].wait()
    count = count_ref[0]
    cnt1[0] = jnp.full(cnt1.shape[1:], count, jnp.int32)
    pl.semaphore_wait(barrier, len(friends))

    for d in range(1, PLANE):
        send(None, c1, d)

    @pl.when(core == 0)
    def _():
        send(0, pair_to1)

    @pl.when(core == 1)
    def _():
        send(1, pair_to0)

    send(None, head, 0)
    load.wait()
    tail_pick = pick(onehot(trows, ing.shape[0], count - trows))
    tail_s[0] = dot(tail_pick, ing[:, 0:hcols]).astype(BF16)
    send(None, tail, 0)
    total = cnt1[0]
    inside = jnp.zeros_like(total)
    for d in range(1, PLANE):
        c1(d).wait_recv()
        total += cnt1[d]
        inside += jnp.where(lax.rem(p + PLANE - d, PLANE) < p, cnt1[d], 0)
    cnt2[0] = total
    for d in range(1, half):
        send(None, c2, d)

    @pl.when(core == 0)
    def _():
        own_a().wait()
        pair_to0().wait_recv()
        send(0, ua, 1, 0)
        send(0, da, 1, 0)
        for d in range(1, NY):
            send(0, ya, d)

    @pl.when(core == 1)
    def _():
        own_b().wait()
        pair_to1().wait_recv()
        for piece in range(2):
            for way, ring in enumerate((ub, db)):
                if goes(way, 1, piece):
                    send(1, ring, 1, piece)
        send(1, yu, 0)
        send(1, yd, 0)

    tail_s[1] = dot(tail_pick, ing[:, hcols:]).astype(BF16)
    send(None, head, 1)
    send(None, tail, 1)

    def step_a(st):
        if st == 0:
            for j in range(1, NY):
                ya(j).wait_recv()
                if half > 1 or j < NY // 2:
                    send(0, ua, 1, j)
                if half > 1 or j >= NY // 2:
                    send(0, da, 1, j)
            send(0, pass_a, 0)
            return
        for j in range(NY):
            if st < half or j < NY // 2:
                ua(st, j).wait_recv()
            if st + 1 < half or (st + 1 == half and j < NY // 2):
                send(0, ua, st + 1, j)
            if st < half or j >= NY // 2:
                da(st, j).wait_recv()
            if st + 1 < half or (st + 1 == half and j >= NY // 2):
                send(0, da, st + 1, j)
        for t in planes(st):
            send(0, pass_a, t)

    def step_b(st):
        if st <= half:
            for piece in range(2):
                for way, ring in enumerate((ub, db)):
                    if goes(way, st, piece):
                        ring(st, piece).wait_recv()
                    if goes(way, st + 1, piece):
                        send(1, ring, st + 1, piece)
            for t in planes(st):
                send(1, yu, t)
                send(1, yd, t)
        if 2 <= st <= half + 2:
            for t in planes(st - 2):
                yu(t).wait_recv()
                yd(t).wait_recv()
                send(1, yf, t)
        if 3 <= st <= half + 3:
            for t in planes(st - 3):
                yf(t).wait_recv()
                send(1, pass_b, t)

    @pl.when(core == 1)
    def _():
        step_b(1)

    group = cnt2[0]
    for d in range(1, half):
        c2(d).wait_recv()
        group += cnt2[d]
        inside += jnp.where(lax.rem(zlow + half - d, half) < zlow, cnt2[d], 0)
    inside += jnp.where(z >= half, rows_total - group, 0)
    shift = s * tokens - inside[0:1, 0:1]
    top = pick(onehot(trows, trows + 2 * hrows, hrows + shift))
    sel_t[...] = top[:, :trows]
    sel_o[...] = top[:, trows:]
    slot = lax.broadcasted_iota(jnp.int32, (hrows, 3 * hrows), 1)
    sel_b[...] = pick(onehot(hrows, 3 * hrows, hrows + shift) & (slot < count))
    sel_h[...] = pick(onehot(hrows, hrows, hrows + shift - count))

    def assemble(h):
        tail(h).wait_recv()
        head(h).wait_recv()
        cols = slice(h * hcols, (h + 1) * hcols)
        spot = x * 2 + h
        feat[spot, 0:trows] = (
            dot(sel_t[...], tail_r[h]) + dot(sel_o[...], ing[0:2 * hrows, cols])).astype(BF16)
        feat[spot, trows:trows + hrows] = (
            dot(sel_b[...], ing[0:3 * hrows, cols]) + dot(sel_h[...], head_r[h])).astype(BF16)
        for r in range(4):
            send(None, xr, h, r)
            send(None, xl, h, r)

    units = [(h, r) for h in range(2) for r in range(4)]

    def xforward(h, r):
        xr(h, r).wait_recv()
        xl(h, r).wait_recv()
        send(None, xf, h, r)

    waiting = list(units)

    @pl.when(core == 0)
    def _():
        step_a(0)

    for st in range(1, half + 1):
        if st <= 2:
            assemble(st - 1)

        @pl.when(core == 0)
        def _():
            step_a(st)

        @pl.when(core == 1)
        def _():
            step_b(st + 1)

        if st == 3 or half < 3 and st == half:
            for copy in small[1:]:
                copy.wait()
            row = lax.broadcasted_iota(jnp.int32, (128, 128), 0)
            col = lax.broadcasted_iota(jnp.int32, (128, 128), 1)
            lens = lens_ref[...].astype(F32)
            lens_col = jnp.sum(jnp.where(row == col, lens, 0.0), axis=1, keepdims=True)
            starts = jnp.sum(jnp.where(row < col, lens_col, 0.0), axis=0, keepdims=True)
            places = (s * tokens + lax.broadcasted_iota(jnp.int32, (tokens, 128), 0)).astype(F32)
            since = places - starts
            age = jnp.min(jnp.where(since >= 0.0, since, 1e9), axis=1, keepdims=True)
            for lag in range(1, 4):
                keep[lag - 1] = jnp.broadcast_to(jnp.where(age >= lag, 1.0, 0.0), (tokens, 128))
        if st >= 2 and waiting:
            xforward(*waiting.pop(0))
    while waiting:
        xforward(*waiting.pop(0))

    @pl.when(core == 0)
    def _():
        for t in range(nz):
            pass_b(t).wait_recv()

    @pl.when(core == 1)
    def _():
        step_b(half + 2)
        step_b(half + 3)
        for t in range(nz):
            pass_a(t).wait_recv()

    def project(first, rows, rels, fresh, last):
        def columns(w, base, width, number):
            @pl.loop(0, number)
            def _(n):
                from_ = pl.ds(pl.multiple_of(n * width, width), width)
                to = pl.ds(pl.multiple_of(base + n * width, 128), width)
                value = None if fresh else proj[first:first + rows, to]
                for rel in rels:
                    source = xof(rel)
                    for h in range(2):
                        deep = pl.ds(pl.multiple_of(source * per_x + h * hcols, hcols), hcols)
                        term = dot(feat[source * 2 + h, first:first + rows], w[deep, from_])
                        value = term if value is None else value + term
                if last:
                    value = value.astype(BF16).astype(F32)
                proj[first:first + rows, to] = value

        columns(wa, 0, ca, 1)
        columns(wb, ca, cb, 1)

    def activate(first, rows):
        block = min(64, rows)

        @pl.loop(0, rows // block)
        def _(n):
            base = pl.multiple_of(first + n * block, block)
            here = pl.ds(base, block)
            for c in range((ca + cb) // 128):
                cols = slice(c * 128, (c + 1) * 128)
                window = proj[pl.ds(pl.multiple_of(base + LEAD - 8, 8), block + 8), cols]
                value = bias_ref[cols].reshape(1, 128) + taps_ref[0:1, cols] * window[8:]
                for lag in range(1, 4):
                    value += taps_ref[lag:lag + 1, cols] * window[8 - lag:8 - lag + block] * keep[lag - 1, here]
                value = 0.5 * value
                outv[here, cols] = (value + value * jnp.tanh(value)).astype(BF16)

        rows_ = pl.ds(first, rows)
        copy = pltpu.make_async_copy(outv.at[rows_], out.at[rows_], lsem.at[2 + first // hrows])
        copy.start()
        return copy

    for h in range(2):
        for r in range(2):
            xf(h, r).wait_recv()
    project(0, trows, (0, -1, 1, 2), True, True)
    copy0 = activate(0, hrows)
    project(trows, hrows, (0, -1, 1), True, False)
    for h in range(2):
        for r in range(2, 4):
            xf(h, r).wait_recv()
    project(trows, hrows, (2,), False, True)
    copy1 = activate(hrows, hrows)

    for make, args in sent[None]:
        make(*args).wait_send()

    @pl.when(core == 0)
    def _():
        for make, args in sent[0]:
            make(*args).wait_send()

    @pl.when(core == 1)
    def _():
        for make, args in sent[1]:
            make(*args).wait_send()

    copy0.wait()
    copy1.wait()


def body(ingest, ingest_count, doc_lengths, in_weight, conv_weight, conv_bias):
    nz = lax.axis_size("seq") // PLANE
    table = names(nz)
    tokens = ingest.shape[0] // 2
    hrows, trows = tokens // 2, tokens // 2 + LEAD
    depth, channels = in_weight.shape
    features = ingest.shape[1]
    hcols = features // 2
    ca = channels * 2 // 5 // 128 * 128
    cb = channels - ca
    total_depth = nz * PLANE * depth
    hbm = pl.BlockSpec(memory_space=pltpu.HBM)
    flops = 2 * tokens * total_depth * channels
    return pl.pallas_call(
        functools.partial(kernel, nz, table, nz * PLANE * tokens),
        out_shape=jax.ShapeDtypeStruct((tokens, channels), BF16),
        in_specs=[hbm] * 6,
        out_specs=hbm,
        scratch_shapes=[
            pltpu.SMEM((1,), jnp.int32),
            pltpu.VMEM((1, 128), jnp.int32),
            pltpu.VMEM(conv_weight.shape, F32),
            pltpu.VMEM(conv_bias.shape, F32),
            pltpu.VMEM(ingest.shape, BF16),
            pltpu.VMEM((2, trows, hcols), BF16),
            pltpu.VMEM((2, trows, hcols), BF16),
            pltpu.VMEM((2, hrows, hcols), BF16),
            pltpu.VMEM((total_depth, ca), BF16),
            pltpu.VMEM((total_depth, cb), BF16),
            pltpu.VMEM((2 * NX, LEAD + tokens, hcols), BF16),
            pltpu.VMEM((LEAD + tokens, channels), F32),
            pltpu.VMEM((3, tokens, 128), F32),
            pltpu.VMEM((PLANE, 8, 128), jnp.int32),
            pltpu.VMEM((nz // 2, 8, 128), jnp.int32),
            pltpu.VMEM((trows, trows), BF16),
            pltpu.VMEM((trows, 2 * hrows), BF16),
            pltpu.VMEM((hrows, 3 * hrows), BF16),
            pltpu.VMEM((hrows, hrows), BF16),
            pltpu.VMEM((tokens, channels), BF16),
            pltpu.SemaphoreType.DMA((8,)),
            pltpu.SemaphoreType.DMA((len(table),)),
            pltpu.SemaphoreType.DMA((len(table),)),
        ],
        compiler_params=pltpu.CompilerParams(
            collective_id=0, has_side_effects=True, vmem_limit_bytes=60 * 1024 * 1024),
        cost_estimate=pl.CostEstimate(flops=flops, bytes_accessed=20 << 20, transcendentals=tokens * channels),
    )(ingest_count, doc_lengths.reshape(1, -1), conv_weight, conv_bias, ingest, in_weight)


def solution(mesh):
    placed = (P("seq", "ch"), P("seq"), P(), P("seq", "ch"), P(None, "ch"), P("ch"))
    return jax.shard_map(
        body, mesh=mesh, in_specs=placed, out_specs=P("seq", "ch"), check_vma=False
    )
```

```python
import functools

import jax
import jax.numpy as jnp
from jax import lax
from jax.experimental import pallas as pl
from jax.experimental.pallas import tpu as pltpu
from jax.sharding import PartitionSpec as P

MESH = pl.DeviceIdType.MESH
F32 = jnp.float32
BF16 = jnp.bfloat16
NY, NX = 4, 4
PLANE = 2 * NY
LEAD = 16


def onehot(rows, columns, shift):
    q = lax.broadcasted_iota(jnp.int32, (rows, columns), 0)
    k = lax.broadcasted_iota(jnp.int32, (rows, columns), 1)
    return k - q == shift


def pick(mask):
    return jnp.where(mask, 1.0, 0.0).astype(BF16)


def dot(a, b):
    return jnp.dot(a, b, preferred_element_type=F32)


def names(nz):
    table, half = {}, nz // 2

    def add(*key):
        table[key] = len(table)

    for d in range(1, PLANE):
        add("c1", d)
    for d in range(1, half):
        add("c2", d)
    add("pair")
    for h in range(2):
        add("tail", h)
        add("head", h)
        for r in range(4):
            add("xr", h, r)
            add("xl", h, r)
            add("xf", h, r)
    for d in range(1, NY):
        add("ya", d)
    for s in range(1, half + 1):
        for j in range(NY):
            add("ua", s, j)
            add("da", s, j)
        for piece in range(2):
            add("ub", s, piece)
            add("db", s, piece)
    for t in range(nz):
        add("yu", t)
        add("yd", t)
        add("yf", t)
        add("pass", t)
    return table


def kernel(nz, table, rows_total, count_hbm, lens_hbm, taps_hbm, bias_hbm, ingest, weight, out,
           count_ref, lens_ref, taps_ref, bias_ref, ing, tail_s, tail_r, head_r, wa, wb, feat, proj, keep, cnt1, cnt2,
           sel_t, sel_o, sel_b, sel_h, outv, lsem, ssem, rsem):
    half = nz // 2
    tokens = outv.shape[0]
    hrows = tokens // 2
    trows = hrows + LEAD
    unit = tokens // 4
    depth, ca = weight.shape[0], wa.shape[1]
    cb = wb.shape[1]
    hcols = feat.shape[2]
    pair_rows = 2 * depth
    plane_rows = PLANE * depth
    per_x = nz * plane_rows // NX

    s = lax.axis_index("seq")
    x = lax.axis_index("ch")
    core = lax.rem(s, 2)
    p = lax.rem(s, PLANE)
    y = p // 2
    z = s // PLANE
    count_devices = nz * PLANE

    def at(zz, yy, cc):
        return {"seq": (zz * NY + yy) * 2 + cc, "ch": x}

    def zof(d):
        return lax.rem(z + (d + 2 * nz), nz)

    zlow = lax.rem(z, half)

    def zpeer(d):
        return z - zlow + lax.rem(zlow + d, half)

    def yof(d):
        return lax.rem(y + (d + 2 * NY), NY)

    def xof(d):
        return lax.rem(x + (d + 2 * NX), NX)

    right = {"seq": lax.rem(s + 1, count_devices), "ch": x}
    left = {"seq": lax.rem(s + count_devices - 1, count_devices), "ch": x}
    sibling = {"seq": s + 1 - 2 * core, "ch": x}
    far = {"seq": lax.rem(s + count_devices - 1 + 2 * core, count_devices), "ch": x}
    xright = {"seq": s, "ch": xof(1)}
    xleft = {"seq": s, "ch": xof(-1)}

    def blk(zz, yy):
        return pl.ds(pl.multiple_of((zz * NY + yy) * pair_rows, pair_rows), pair_rows)

    def plane(zz):
        return pl.ds(pl.multiple_of(zz * plane_rows, plane_rows), plane_rows)

    def rc(key, src, dst, device):
        i = table[key]
        return pltpu.make_async_remote_copy(
            src_ref=src, dst_ref=dst, send_sem=ssem.at[i], recv_sem=rsem.at[i],
            device_id=device, device_id_type=MESH)

    sent = {None: [], 0: [], 1: []}

    def send(who, make, *args):
        make(*args).start()
        sent[who].append((make, args))

    def c1(d):
        peer = lax.rem(p + d, PLANE)
        return rc(("c1", d), cnt1.at[0], cnt1.at[d], {"seq": z * PLANE + peer, "ch": x})

    def c2(d):
        return rc(("c2", d), cnt2.at[0], cnt2.at[d], {"seq": zpeer(d) * PLANE + p, "ch": x})

    mine = pl.ds(pl.multiple_of(s * depth, depth), depth)

    def pair_to0():
        return rc(("pair",), weight.at[:, 0:ca], wa.at[mine], sibling)

    def pair_to1():
        return rc(("pair",), weight.at[:, ca:], wb.at[mine], sibling)

    def tail(h):
        return rc(("tail", h), tail_s.at[h], tail_r.at[h], right)

    def head(h):
        return rc(("head", h), ingest.at[0:hrows, h * hcols:(h + 1) * hcols], head_r.at[h], left)

    def xrows(r):
        return pl.ds(0, LEAD + unit) if r == 0 else pl.ds(LEAD + r * unit, unit)

    def xcopy(kind, h, r, source, device):
        block = feat.at[source * 2 + h, xrows(r)]
        return rc((kind, h, r), block, block, device)

    def xr(h, r):
        return xcopy("xr", h, r, x, xright)

    def xl(h, r):
        return xcopy("xl", h, r, x, xleft)

    def xf(h, r):
        if r % 2 == 0:
            return xcopy("xf", h, r, xof(-1), xright)
        return xcopy("xf", h, r, xof(1), xleft)

    def ya(d):
        block = wa.at[blk(z, y)]
        return rc(("ya", d), block, block, at(z, yof(d), 0))

    def ua(st, j):
        block = wa.at[blk(zof(1 - st), yof(-j))]
        return rc(("ua", st, j), block, block, at(zof(1), y, 0))

    def da(st, j):
        block = wa.at[blk(zof(st - 1), yof(-j))]
        return rc(("da", st, j), block, block, at(zof(-1), y, 0))

    def part(zz, yy, piece):
        first = (zz * NY + yy) * pair_rows + piece * depth
        return pl.ds(pl.multiple_of(first, depth), depth)

    def ub(st, piece):
        block = wb.at[part(zof(1 - st), y, piece)]
        return rc(("ub", st, piece), block, block, at(zof(1), y, 1))

    def db(st, piece):
        block = wb.at[part(zof(st - 1), y, piece)]
        return rc(("db", st, piece), block, block, at(zof(-1), y, 1))

    def goes(way, st, piece):
        return st < half or (st == half and piece == way)

    def yu(t):
        block = wb.at[blk(zof(-t), y)]
        return rc(("yu", t), block, block, at(z, yof(1), 1))

    def yd(t):
        block = wb.at[blk(zof(-t), y)]
        return rc(("yd", t), block, block, at(z, yof(-1), 1))

    def yf(t):
        step = 1 if t % 2 == 0 else -1
        block = wb.at[blk(zof(-t), yof(-step))]
        return rc(("yf", t), block, block, at(z, yof(step), 1))

    def pass_a(t):
        block = wa.at[plane(zof(-t))]
        return rc(("pass", t), block, block, sibling)

    def pass_b(t):
        block = wb.at[plane(zof(-t))]
        return rc(("pass", t), block, block, sibling)

    def planes(st):
        return [st] if st in (0, half) else [st, nz - st]

    load = pltpu.make_async_copy(ingest, ing, lsem.at[0])
    small = [pltpu.make_async_copy(a, b, lsem.at[4 + i]) for i, (a, b) in enumerate(
        ((count_hbm, count_ref), (lens_hbm, lens_ref), (taps_hbm, taps_ref), (bias_hbm, bias_ref)))]
    small[0].start()
    load.start()

    def own_a():
        return pltpu.make_async_copy(weight.at[:, 0:ca], wa.at[mine], lsem.at[1])

    def own_b():
        return pltpu.make_async_copy(weight.at[:, ca:], wb.at[mine], lsem.at[1])

    @pl.when(core == 0)
    def _():
        own_a().start()

    @pl.when(core == 1)
    def _():
        own_b().start()

    barrier = pltpu.get_barrier_semaphore()
    friends = [{"seq": zpeer(d) * PLANE + p, "ch": x} for d in range(1, half)]
    friends += [at(zof(1), y, core), at(zof(-1), y, core), far, xright, xleft]
    friends += [{"seq": z * PLANE + lax.rem(p + d, PLANE), "ch": x} for d in range(1, PLANE)]
    for friend in friends:
        pl.semaphore_signal(barrier, inc=1, device_id=friend, device_id_type=MESH)
    for copy in small[1:]:
        copy.start()
    small[0].wait()
    count = count_ref[0]
    cnt1[0] = jnp.full(cnt1.shape[1:], count, jnp.int32)
    pl.semaphore_wait(barrier, len(friends))

    for d in range(1, PLANE):
        send(None, c1, d)

    @pl.when(core == 0)
    def _():
        send(0, pair_to1)

    @pl.when(core == 1)
    def _():
        send(1, pair_to0)

    send(None, head, 0)
    load.wait()
    tail_pick = pick(onehot(trows, ing.shape[0], count - trows))
    tail_s[0] = dot(tail_pick, ing[:, 0:hcols]).astype(BF16)
    send(None, tail, 0)
    total = cnt1[0]
    inside = jnp.zeros_like(total)
    for d in range(1, PLANE):
        c1(d).wait_recv()
        total += cnt1[d]
        inside += jnp.where(lax.rem(p + PLANE - d, PLANE) < p, cnt1[d], 0)
    cnt2[0] = total
    for d in range(1, half):
        send(None, c2, d)

    @pl.when(core == 0)
    def _():
        own_a().wait()
        pair_to0().wait_recv()
        send(0, ua, 1, 0)
        send(0, da, 1, 0)
        for d in range(1, NY):
            send(0, ya, d)

    @pl.when(core == 1)
    def _():
        own_b().wait()
        pair_to1().wait_recv()
        for piece in range(2):
            for way, ring in enumerate((ub, db)):
                if goes(way, 1, piece):
                    send(1, ring, 1, piece)
        send(1, yu, 0)
        send(1, yd, 0)

    tail_s[1] = dot(tail_pick, ing[:, hcols:]).astype(BF16)
    send(None, head, 1)
    send(None, tail, 1)

    def step_a(st):
        if st == 0:
            for j in range(1, NY):
                ya(j).wait_recv()
                if half > 1 or j < NY // 2:
                    send(0, ua, 1, j)
                if half > 1 or j >= NY // 2:
                    send(0, da, 1, j)
            send(0, pass_a, 0)
            return
        for j in range(NY):
            if st < half or j < NY // 2:
                ua(st, j).wait_recv()
            if st + 1 < half or (st + 1 == half and j < NY // 2):
                send(0, ua, st + 1, j)
            if st < half or j >= NY // 2:
                da(st, j).wait_recv()
            if st + 1 < half or (st + 1 == half and j >= NY // 2):
                send(0, da, st + 1, j)
        for t in planes(st):
            send(0, pass_a, t)

    def step_b(st):
        if st <= half:
            for piece in range(2):
                for way, ring in enumerate((ub, db)):
                    if goes(way, st, piece):
                        ring(st, piece).wait_recv()
                    if goes(way, st + 1, piece):
                        send(1, ring, st + 1, piece)
            for t in planes(st):
                send(1, yu, t)
                send(1, yd, t)
        if 2 <= st <= half + 2:
            for t in planes(st - 2):
                yu(t).wait_recv()
                yd(t).wait_recv()
                send(1, yf, t)
        if 3 <= st <= half + 3:
            for t in planes(st - 3):
                yf(t).wait_recv()
                send(1, pass_b, t)

    @pl.when(core == 1)
    def _():
        step_b(1)

    group = cnt2[0]
    for d in range(1, half):
        c2(d).wait_recv()
        group += cnt2[d]
        inside += jnp.where(lax.rem(zlow + half - d, half) < zlow, cnt2[d], 0)
    inside += jnp.where(z >= half, rows_total - group, 0)
    shift = s * tokens - inside[0:1, 0:1]
    top = pick(onehot(trows, trows + 2 * hrows, hrows + shift))
    sel_t[...] = top[:, :trows]
    sel_o[...] = top[:, trows:]
    slot = lax.broadcasted_iota(jnp.int32, (hrows, 3 * hrows), 1)
    sel_b[...] = pick(onehot(hrows, 3 * hrows, hrows + shift) & (slot < count))
    sel_h[...] = pick(onehot(hrows, hrows, hrows + shift - count))

    def assemble(h):
        tail(h).wait_recv()
        head(h).wait_recv()
        cols = slice(h * hcols, (h + 1) * hcols)
        spot = x * 2 + h
        feat[spot, 0:trows] = (
            dot(sel_t[...], tail_r[h]) + dot(sel_o[...], ing[0:2 * hrows, cols])).astype(BF16)
        feat[spot, trows:trows + hrows] = (
            dot(sel_b[...], ing[0:3 * hrows, cols]) + dot(sel_h[...], head_r[h])).astype(BF16)
        for r in range(4):
            send(None, xr, h, r)
            send(None, xl, h, r)

    units = [(h, r) for h in range(2) for r in range(4)]

    def xforward(h, r):
        xr(h, r).wait_recv()
        xl(h, r).wait_recv()
        send(None, xf, h, r)

    waiting = list(units)

    @pl.when(core == 0)
    def _():
        step_a(0)

    for st in range(1, half + 1):
        if st <= 2:
            assemble(st - 1)

        @pl.when(core == 0)
        def _():
            step_a(st)

        @pl.when(core == 1)
        def _():
            step_b(st + 1)

        if st == 3 or half < 3 and st == half:
            for copy in small[1:]:
                copy.wait()
            row = lax.broadcasted_iota(jnp.int32, (128, 128), 0)
            col = lax.broadcasted_iota(jnp.int32, (128, 128), 1)
            lens = lens_ref[...].astype(F32)
            lens_col = jnp.sum(jnp.where(row == col, lens, 0.0), axis=1, keepdims=True)
            starts = jnp.sum(jnp.where(row < col, lens_col, 0.0), axis=0, keepdims=True)
            places = (s * tokens + lax.broadcasted_iota(jnp.int32, (tokens, 128), 0)).astype(F32)
            since = places - starts
            age = jnp.min(jnp.where(since >= 0.0, since, 1e9), axis=1, keepdims=True)
            for lag in range(1, 4):
                keep[lag - 1] = jnp.broadcast_to(jnp.where(age >= lag, 1.0, 0.0), (tokens, 128))
        if st >= 2 and waiting:
            xforward(*waiting.pop(0))
    while waiting:
        xforward(*waiting.pop(0))

    def multiply(w, base):
        value = None
        for rel in (0, -1, 1):
            source = xof(rel)
            for h in range(2):
                deep = pl.ds(pl.multiple_of(source * per_x + h * hcols, hcols), hcols)
                term = dot(feat[source * 2 + h], w[deep])
                value = term if value is None else value + term
        proj[:, base:base + w.shape[1]] = value

    @pl.when(core == 1)
    def _():
        step_b(half + 2)
        step_b(half + 3)
        for t in range(nz):
            pass_a(t).wait_recv()

    @pl.when(core == 0)
    def _():
        for t in range(nz):
            pass_b(t).wait_recv()

    multiply(wa, 0)
    multiply(wb, ca)

    def finish(first, rows):
        source = xof(2)
        for w, base in ((wa, 0), (wb, ca)):
            to = slice(base, base + w.shape[1])
            value = proj[first:first + rows, to]
            for h in range(2):
                deep = pl.ds(pl.multiple_of(source * per_x + h * hcols, hcols), hcols)
                value += dot(feat[source * 2 + h, first:first + rows], w[deep])
            proj[first:first + rows, to] = value.astype(BF16).astype(F32)

    def activate(first, rows):
        block = min(64, rows)

        @pl.loop(0, rows // block)
        def _(n):
            base = pl.multiple_of(first + n * block, block)
            here = pl.ds(base, block)
            for c in range((ca + cb) // 128):
                cols = slice(c * 128, (c + 1) * 128)
                window = proj[pl.ds(pl.multiple_of(base + LEAD - 8, 8), block + 8), cols]
                value = bias_ref[cols].reshape(1, 128) + taps_ref[0:1, cols] * window[8:]
                for lag in range(1, 4):
                    value += taps_ref[lag:lag + 1, cols] * window[8 - lag:8 - lag + block] * keep[lag - 1, here]
                value = 0.5 * value
                outv[here, cols] = (value + value * jnp.tanh(value)).astype(BF16)

        rows_ = pl.ds(first, rows)
        copy = pltpu.make_async_copy(outv.at[rows_], out.at[rows_], lsem.at[2 + first // hrows])
        copy.start()
        return copy

    for h in range(2):
        for r in range(2):
            xf(h, r).wait_recv()
    finish(0, trows)
    copy0 = activate(0, hrows)
    for h in range(2):
        for r in range(2, 4):
            xf(h, r).wait_recv()
    finish(trows, hrows)
    copy1 = activate(hrows, hrows)

    for make, args in sent[None]:
        make(*args).wait_send()

    @pl.when(core == 0)
    def _():
        for make, args in sent[0]:
            make(*args).wait_send()

    @pl.when(core == 1)
    def _():
        for make, args in sent[1]:
            make(*args).wait_send()

    copy0.wait()
    copy1.wait()


def body(ingest, ingest_count, doc_lengths, in_weight, conv_weight, conv_bias):
    nz = lax.axis_size("seq") // PLANE
    table = names(nz)
    tokens = ingest.shape[0] // 2
    hrows, trows = tokens // 2, tokens // 2 + LEAD
    depth, channels = in_weight.shape
    features = ingest.shape[1]
    hcols = features // 2
    ca = channels * 2 // 5 // 128 * 128
    cb = channels - ca
    total_depth = nz * PLANE * depth
    hbm = pl.BlockSpec(memory_space=pltpu.HBM)
    flops = 2 * tokens * total_depth * channels
    return pl.pallas_call(
        functools.partial(kernel, nz, table, nz * PLANE * tokens),
        out_shape=jax.ShapeDtypeStruct((tokens, channels), BF16),
        in_specs=[hbm] * 6,
        out_specs=hbm,
        scratch_shapes=[
            pltpu.SMEM((1,), jnp.int32),
            pltpu.VMEM((1, 128), jnp.int32),
            pltpu.VMEM(conv_weight.shape, F32),
            pltpu.VMEM(conv_bias.shape, F32),
            pltpu.VMEM(ingest.shape, BF16),
            pltpu.VMEM((2, trows, hcols), BF16),
            pltpu.VMEM((2, trows, hcols), BF16),
            pltpu.VMEM((2, hrows, hcols), BF16),
            pltpu.VMEM((total_depth, ca), BF16),
            pltpu.VMEM((total_depth, cb), BF16),
            pltpu.VMEM((2 * NX, LEAD + tokens, hcols), BF16),
            pltpu.VMEM((LEAD + tokens, channels), F32),
            pltpu.VMEM((3, tokens, 128), F32),
            pltpu.VMEM((PLANE, 8, 128), jnp.int32),
            pltpu.VMEM((nz // 2, 8, 128), jnp.int32),
            pltpu.VMEM((trows, trows), BF16),
            pltpu.VMEM((trows, 2 * hrows), BF16),
            pltpu.VMEM((hrows, 3 * hrows), BF16),
            pltpu.VMEM((hrows, hrows), BF16),
            pltpu.VMEM((tokens, channels), BF16),
            pltpu.SemaphoreType.DMA((8,)),
            pltpu.SemaphoreType.DMA((len(table),)),
            pltpu.SemaphoreType.DMA((len(table),)),
        ],
        compiler_params=pltpu.CompilerParams(
            collective_id=0, has_side_effects=True, vmem_limit_bytes=60 * 1024 * 1024),
        cost_estimate=pl.CostEstimate(flops=flops, bytes_accessed=20 << 20, transcendentals=tokens * channels),
    )(ingest_count, doc_lengths.reshape(1, -1), conv_weight, conv_bias, ingest, in_weight)


def solution(mesh):
    placed = (P("seq", "ch"), P("seq"), P(), P("seq", "ch"), P(None, "ch"), P("ch"))
    return jax.shard_map(
        body, mesh=mesh, in_specs=placed, out_specs=P("seq", "ch"), check_vma=False
    )
```
